512 devices in a mesh: phase: 4 (over x), expert: 32 (over z_hi, y, core), tensor: 4 (over z_lo).
Axes of the slice: x: 4, y: 4, z: 16 (z_hi: 4, z_lo: 4; z = z_hi * 4 + z_lo), core: 2. Of those that a mesh axis runs over, the one named last changes fastest.
Arguments:
- forward_routes: int32 [4, 2048, 6], P('phase', 'expert'), may hold values from 0 to 95, all different within a row; in each aligned block of 64 rows (0 to 63, 64 to 127, ..., all dimensions but the last counted through in order) at most 6 rows name the same one
- forward_gates: float32 [4, 2048, 6], P('phase', 'expert'), may hold values from 0.05 to 1
- hidden_rows: bfloat16 [4, 96, 32, 6, 1024], P('phase', 'expert', None, None, 'tensor'), may hold values from -6 to 6
- down_weight: bfloat16 [4, 96, 1024, 2560], P('phase', 'expert', 'tensor'), may hold values from -0.1875 to 0.1875
- shared_hidden: bfloat16 [4, 2048, 1536], P('phase', 'expert', 'tensor'), may hold values from -6 to 6
- shared_weight: bfloat16 [4, 1536, 2560], P('phase', 'tensor', 'expert'), may hold values from -0.15625 to 0.15625
- backward_routes: int32 [4, 2048, 6], P('phase', 'expert'), may hold values from 0 to 95, all different within a row; in each aligned block of 64 rows (0 to 63, 64 to 127, ..., all dimensions but the last counted through in order) at most 6 rows name the same one
- backward_gates: float32 [4, 2048, 6], P('phase', 'expert'), may hold values from 0.05 to 1
- cotangent: bfloat16 [4, 2048, 2560], P('phase', 'expert', 'tensor'), may hold values from -6 to 6
Outputs:
- forward_next: bfloat16 [4, 2048, 2560], P('phase', 'expert', 'tensor')
- hidden_grad: bfloat16 [4, 96, 32, 6, 1024], P('phase', 'expert', None, None, 'tensor')
- shared_grad: bfloat16 [4, 2048, 1536], P('phase', 'expert', 'tensor')
The draws below stay inside these ranges and needn't reach their ends.
Inputs may be any that keep to these rules, and one draw needn't show every extreme that they name: `forward_routes`: each token names 6 different experts. The tokens of one token group (the 64 rows of one device) name any one expert 6 times at most, and some group reaches that. `backward_routes`: as for forward_routes.
All inputs are finite; a program needn't handle non-finite values.
Results may differ from the reference program's by a relative error of at most 0.0049.
Values may be sent and summed in bfloat16 or wider, within the bound.
No kernel may reach another device: no remote copies, remote signals or barrier semaphores. Data moves between devices by JAX's collectives and lax.ppermute only.
A program may use at most 64 MiB of HBM per device.

```python
import math
import jax
import jax.numpy as jnp
import numpy as np
from jax import lax

D = 2560
HID = 1024
HS = 1536
TOPK = 6
TOK_DEV = 64
SECTIONS = 4
GROUPS = 32
HPARTS = 4
EXPERTS = 96
TOKENS = 2048
MOST = 6


def shard_levels(own_key, extent, split, low, top_value):
    def one(dim, blocks):
        heights = jax.random.uniform(jax.random.fold_in(jax.random.fold_in(own_key, 6), dim), (blocks,), jnp.float32, low / len(split), top_value / len(split))
        return jnp.repeat(jnp.exp(heights), extent[dim] // blocks).reshape((-1,) + (1,) * (len(extent) - dim - 1))

    loudness = one(*split[0])
    for cut in split[1:]:
        loudness = loudness * one(*cut)
    return loudness


def deal_out(rng, own, number, rows, number_of, top, limit, skew):
    ranking = jax.random.permutation(rng, number_of)
    crowded, ordinary = shares(number_of, rows * top, limit, skew, True), shares(number_of, rows * top, limit, skew, False)
    places = jnp.arange(number_of)

    def named(tallies, offset_by):
        used = int((tallies > 0).sum())
        fixed = max(1, used // 4)
        moved = fixed + (places - fixed + offset_by * (used - fixed)) % max(1, number_of - fixed)
        return jnp.zeros((number_of,), jnp.int32).at[ranking[jnp.where(places < fixed, places, moved)]].set(jnp.asarray(tallies, jnp.int32))

    tallies = jnp.where(number % 4 == 0, named(crowded, number // 4), named(ordinary, number - number // 4 - 1))
    mixed = jax.random.permutation(jax.random.fold_in(own, 3), number_of)
    giver, taker = mixed[0:number_of // 2 * 2:2], mixed[1:number_of // 2 * 2:2]
    room = jnp.minimum(tallies[giver] - 1, limit - tallies[taker]) // 2
    room = jnp.where((giver == ranking[0]) | (taker == ranking[0]) | (tallies[taker] == 0), 0, jnp.maximum(room, 0))
    moved = jax.random.randint(jax.random.fold_in(own, 4), (number_of // 2,), 0, 1 << 20) % (room + 1)
    tallies = tallies.at[giver].add(-moved).at[taker].add(moved)
    labels = jnp.searchsorted(jnp.cumsum(tallies), jnp.arange(rows * top), side="right").astype(jnp.int32)
    listing = labels.reshape(top, rows).T
    listing = listing[jax.random.permutation(jax.random.fold_in(own, 1), rows)]
    offset_by = jax.random.randint(jax.random.fold_in(own, 2), (rows, 1), 0, top)
    return jnp.take_along_axis(listing, (jnp.arange(top)[None, :] + offset_by) % top, axis=1)


def shares(amount, total, bound, lean, full):
    loads = [(1 << 20) // math.isqrt(rank ** lean) + 1 for rank in range(1, amount + 1)]
    largest = bound if full else min(bound, max(-(-total // amount), total * loads[0] // sum(loads)))
    least = 1 if total - largest >= amount - 1 else 0
    counts, spare = [largest] + [least] * (amount - 1), total - largest - least * (amount - 1)
    while spare > 0:
        free = [i for i in range(1, amount) if counts[i] < largest] or [i for i in range(1, amount) if counts[i] < bound]
        whole, left = sum([loads[i] for i in free]), spare
        for i in free:
            extra = min(bound - counts[i], max(1, left * loads[i] // whole), spare)
            counts[i] = counts[i] + extra
            spare = spare - extra
    return np.array(counts)


def normal_values(own_key, shape, width, limit, split=(), kind=jnp.bfloat16):
    level = shard_levels(own_key, shape, split, -0.22, 0.18) if split else 1.0
    array = jax.random.normal(own_key, shape, jnp.float32) * width * level
    return jnp.minimum(jnp.maximum(array, -limit), limit).astype(kind)


def setup_inputs(seed: int = 0) -> dict:
    key_list = jax.random.split(jax.random.key(seed), 10)
    forward_routes_keys = jax.random.split(jax.random.fold_in(key_list[0], 1), SECTIONS * TOKENS // TOK_DEV)
    forward_routes_turns = jax.random.permutation(jax.random.fold_in(key_list[0], 3), SECTIONS * TOKENS // TOK_DEV)
    forward_routes = jax.vmap(lambda own, number: deal_out(jax.random.fold_in(key_list[0], 2), own, number, TOK_DEV, EXPERTS, TOPK, MOST, 2))(forward_routes_keys, forward_routes_turns).reshape((SECTIONS, TOKENS, TOPK))
    forward_gates = jnp.clip(jnp.exp(math.log(1.0) - 2.9957323 * jax.random.uniform(key_list[1], (SECTIONS, TOKENS, TOPK), jnp.float32) ** shard_levels(key_list[1], (SECTIONS, TOKENS, TOPK), ((0, 4), (1, 32)), -0.2, 0.2)), 0.05, 1.0)
    hidden_rows = normal_values(key_list[2], (SECTIONS, EXPERTS, GROUPS, MOST, HID), 1.0, 6.0, ((0, 4), (1, 32), (4, 4)))
    down_weight = normal_values(key_list[3], (SECTIONS, EXPERTS, HID, D), HID ** -0.5, 0.1875, ((0, 4), (1, 32), (2, 4)))
    shared_hidden = normal_values(key_list[4], (SECTIONS, TOKENS, HS), 1.0, 6.0, ((0, 4), (1, 32), (2, 4)))
    shared_weight = normal_values(key_list[5], (SECTIONS, HS, D), HS ** -0.5, 0.15625, ((0, 4), (1, 4), (2, 32)))
    backward_routes_keys = jax.random.split(jax.random.fold_in(key_list[6], 1), SECTIONS * TOKENS // TOK_DEV)
    backward_routes_turns = jax.random.permutation(jax.random.fold_in(key_list[6], 3), SECTIONS * TOKENS // TOK_DEV)
    backward_routes = jax.vmap(lambda own, number: deal_out(jax.random.fold_in(key_list[6], 2), own, number, TOK_DEV, EXPERTS, TOPK, MOST, 2))(backward_routes_keys, backward_routes_turns).reshape((SECTIONS, TOKENS, TOPK))
    backward_gates = jnp.clip(jnp.exp(math.log(1.0) - 2.9957323 * jax.random.uniform(key_list[7], (SECTIONS, TOKENS, TOPK), jnp.float32) ** shard_levels(key_list[7], (SECTIONS, TOKENS, TOPK), ((0, 4), (1, 32)), -0.2, 0.2)), 0.05, 1.0)
    cotangent = normal_values(key_list[8], (SECTIONS, TOKENS, D), 1.0, 6.0, ((0, 4), (1, 32), (2, 4)))
    return {"forward_routes": forward_routes, "forward_gates": forward_gates, "hidden_rows": hidden_rows, "down_weight": down_weight, "shared_hidden": shared_hidden, "shared_weight": shared_weight, "backward_routes": backward_routes, "backward_gates": backward_gates, "cotangent": cotangent}


def slot_numbers(routes, experts):
    numbers = jnp.arange(experts, dtype=jnp.int32)
    onehot = (routes[:, :, None] == numbers[None, None, :]).astype(jnp.int32)
    per_token = jnp.sum(onehot, axis=1)
    before = jnp.cumsum(per_token, axis=0) - per_token
    return jnp.sum(onehot * before[:, None, :], axis=2)


def block_slots(block_routes):
    return slot_numbers(block_routes, EXPERTS)


def positions(routes):
    blocks = routes.reshape(GROUPS, TOK_DEV, TOPK)
    slot_index = jax.vmap(block_slots)(blocks).reshape(TOKENS, TOPK)
    block_index = (jnp.arange(TOKENS, dtype=jnp.int32) // TOK_DEV)[:, None]
    return ((routes * GROUPS + block_index) * MOST + slot_index).reshape(-1)


def forward_rows(operands):
    hidden_block, matrix = operands
    left_side = hidden_block.reshape(GROUPS * MOST, HPARTS, HID // HPARTS).astype(jnp.float32)
    right_side = matrix.reshape(HPARTS, HID // HPARTS, D).astype(jnp.float32)
    pieces = jnp.einsum("rqh,qhd->rqd", left_side, right_side, precision=lax.Precision.HIGHEST).astype(jnp.bfloat16)
    pieces = lax.optimization_barrier(pieces)
    return jnp.sum(pieces.astype(jnp.float32), axis=1)


def backward_rows(operands):
    sent_block, matrix = operands
    return jnp.dot(sent_block, matrix.T, preferred_element_type=jnp.float32).astype(jnp.bfloat16)


def reference(forward_routes, forward_gates, hidden_rows, down_weight, shared_hidden, shared_weight, backward_routes, backward_gates, cotangent):
    layers = []
    hidden_grads = []
    shared_grads = []
    for section in range(SECTIONS):
        fore_positions = positions(forward_routes[section])
        summed = lax.map(forward_rows, (hidden_rows[section], down_weight[section])).reshape(-1, D)
        picked = summed[fore_positions].reshape(TOKENS, TOPK, D)
        routed = jnp.sum(picked * forward_gates[section][:, :, None], axis=1)
        shared_out = jnp.dot(shared_hidden[section], shared_weight[section], preferred_element_type=jnp.float32)
        layers.append((routed + shared_out).astype(jnp.bfloat16))
        back_positions = positions(backward_routes[section])
        scaled = (backward_gates[section][:, :, None] * cotangent[section][:, None, :].astype(jnp.float32)).astype(jnp.bfloat16)
        outgoing = jnp.zeros((EXPERTS * GROUPS * MOST, D), jnp.bfloat16).at[back_positions].set(scaled.reshape(-1, D))
        expert_grads = lax.map(backward_rows, (outgoing.reshape(EXPERTS, GROUPS * MOST, D), down_weight[section]))
        hidden_grads.append(expert_grads.reshape(EXPERTS, GROUPS, MOST, HID))
        shared_grads.append(jnp.dot(cotangent[section], shared_weight[section].T, preferred_element_type=jnp.float32).astype(jnp.bfloat16))
    forward_next = jnp.roll(jnp.stack(layers), 1, axis=0)
    return forward_next, jnp.stack(hidden_grads), jnp.stack(shared_grads)
```

```python
import functools

import jax
import jax.numpy as jnp
from jax import lax
from jax.experimental import pallas as pl
from jax.experimental.pallas import tpu as pltpu
from jax.sharding import Mesh, PartitionSpec as P

BF, F32 = jnp.bfloat16, jnp.float32
ZHI, YS, CORES, QS = 4, 4, 2, 4
DESTS = YS * CORES
HERE, MOST, TOK, TOP = 3, 6, 64, 6
SLOTS = ZHI * MOST
COLS = DESTS * HERE
ROWS = COLS * SLOTS
FEAT, HID = 640, 256
HSQ, WCOL = 384, 80
TALL = ZHI * TOK
XPAD = 32
BLOCKS = HERE * QS + 2
WIDE = FEAT + HSQ + 128
SEND = FEAT + HSQ
VM = pl.BlockSpec(memory_space=pltpu.VMEM)


def call(body, outs, args, flops=0, name=None):
    out_shape = [jax.ShapeDtypeStruct(s, t) for s, t in outs]
    size = sum(a.size * a.dtype.itemsize for a in (*args, *out_shape))
    return pl.pallas_call(
        body,
        out_shape=out_shape,
        in_specs=[VM] * len(args),
        out_specs=[VM] * len(outs),
        cost_estimate=pl.CostEstimate(flops=flops, bytes_accessed=size, transcendentals=0),
        compiler_params=pltpu.CompilerParams(vmem_limit_bytes=48 * 2**20),
        name=name,
    )(*args)


def iota(shape, dim):
    return lax.broadcasted_iota(jnp.int32, shape, dim)


def dot(a, b, dims=((1,), (0,))):
    return lax.dot_general(a, b, (dims, ((), ())), preferred_element_type=F32)


def split_row(r):
    x = (r * 2731) >> 16
    rest = r - x * SLOTS
    group = (rest * 43) >> 8
    return x, group, rest - group * MOST


def fore_kernel(hidden, weight, columns, out, rows_ref):
    step = pl.program_id(0)
    count = MOST * ZHI * DESTS

    @pl.when((step < 2 * HERE) & (lax.rem(step, 2) == 0))
    def _():
        to, src = iota((count, count), 0), iota((count, count), 1)
        slot, group = src >> 5, src & 31
        zhi, dest = group >> 3, group & 7
        perm = jnp.where(to == (dest * SLOTS + zhi * MOST + slot), 1.0, 0.0).astype(BF)
        rows_ref[...] = dot(perm, hidden[0].reshape(count, HID)).astype(BF)

    @pl.when(step < 2 * HERE)
    def _():
        for q in range(2):
            value = dot(rows_ref[...], weight[0, :, q * FEAT : (q + 1) * FEAT])
            out[:, q] = value.reshape(DESTS, SLOTS, FEAT).astype(BF)

    @pl.when(step == 2 * HERE)
    def _():
        wide = columns[...].astype(F32)
        tiles = [wide[8 * m : 8 * m + 8, 128 * i : 128 * i + 128] for i in range(3) for m in range(10)]
        for b in range(2):
            lanes = [jnp.concatenate(tiles[3 * n : 3 * n + 3], axis=0) for n in range(5 * b, 5 * b + 5)]
            block = jnp.concatenate(lanes, axis=1).astype(BF)
            for d in range(DESTS):
                out[d, b] = block


def unpacked_columns(rows):
    pieces = []
    for d in range(DESTS):
        blocks = [rows[d, BLOCKS - 2 + b].astype(F32) for b in range(2)]
        tiles = [
            blocks[n // 5][8 * m : 8 * m + 8, 128 * (n % 5) : 128 * (n % 5) + 128]
            for n in range(10)
            for m in range(3)
        ]
        lanes = [jnp.concatenate(tiles[10 * i : 10 * i + 10], axis=0) for i in range(3)]
        pieces.append(jnp.concatenate(lanes, axis=1))
    return jnp.concatenate(pieces, axis=0).astype(BF)


def back_kernel(rows, weight, out):
    count = MOST * ZHI * DESTS
    total = jnp.zeros((count, HID), F32)
    for q in range(QS):
        piece = rows[:, 0, q].astype(F32).reshape(count, FEAT).astype(BF)
        total += dot(piece, weight[0, :, q * FEAT : (q + 1) * FEAT], ((1,), (1,)))
    to, src = iota((count, count), 0), iota((count, count), 1)
    slot, group = to >> 5, to & 31
    zhi, dest = group >> 3, group & 7
    perm = jnp.where(src == (dest * SLOTS + zhi * MOST + slot), 1.0, 0.0).astype(BF)
    value = dot(perm, total.astype(BF)).astype(BF)
    out[0] = value.reshape(MOST, ZHI * DESTS, HID)


def select_kernel(whole, cot0, cot1, cot2, cot3, out):
    q = lax.axis_index("tensor")
    meta = whole[:, :, SEND:].astype(F32).reshape(TALL, 128).T
    names = iota((XPAD, TALL), 0) + lax.axis_index("zhi") * COLS
    hit = jnp.zeros((XPAD, TALL), F32)
    gates = [jnp.zeros((XPAD, TALL), F32) for _ in range(3)]
    for k in range(TOP):
        found = jnp.where(meta[6 + k : 7 + k, :].astype(jnp.int32) == names, 1.0, 0.0)
        hit += found
        for i in range(3):
            gates[i] += found * meta[30 + 6 * i + k : 31 + 6 * i + k, :]
    a, b = iota((TALL, TALL), 0), iota((TALL, TALL), 1)
    before = jnp.where((a < b) & ((a >> 6) == (b >> 6)), 1.0, 0.0).astype(BF)
    slot = jnp.where(hit > 0, dot(hit.astype(BF), before), 100.0)
    x, _, _ = split_row(iota((ROWS, XPAD), 0))
    spread = jnp.where(x == iota((ROWS, XPAD), 1), 1.0, 0.0).astype(BF)
    slots = dot(spread, slot.astype(BF))
    gate = sum(dot(spread, g.astype(BF)) for g in gates)
    _, group, want = split_row(iota((ROWS, TALL), 0))
    chosen = (slots == want.astype(F32)) & (group == (iota((ROWS, TALL), 1) >> 6))
    pick = jnp.where(chosen, 1.0, 0.0).astype(BF)
    scale = jnp.sum(jnp.where(chosen, gate, 0.0), axis=1, keepdims=True)
    for i, cot in enumerate((cot0, cot1, cot2, cot3)):
        value = dot(pick, cot[...].reshape(TALL, FEAT)) * scale
        out[:, :, lax.rem(q + i, QS)] = value.reshape(DESTS, HERE, SLOTS, FEAT).astype(BF)


def combine_kernel(whole, rows, own, send1, send2, send3, columns):
    me = lax.axis_index("zhi")
    q = lax.axis_index("tensor")
    meta = whole[:, :, SEND:].astype(F32).reshape(TALL, 128)
    names = iota((TALL, 128), 1) + me * COLS
    hit = jnp.zeros((TALL, 128), F32)
    gates = [jnp.zeros((TALL, 128), F32) for _ in range(3)]
    for k in range(TOP):
        found = jnp.where(meta[:, k : k + 1].astype(jnp.int32) == names, 1.0, 0.0)
        hit += found
        for i in range(3):
            gates[i] += found * meta[:, 12 + 6 * i + k : 13 + 6 * i + k]
    a, b = iota((TALL, TALL), 0), iota((TALL, TALL), 1)
    before = jnp.where((b < a) & ((a >> 6) == (b >> 6)), 1.0, 0.0).astype(BF)
    slot = jnp.where(hit > 0, dot(before, hit.astype(BF)), 100.0)
    x, _, _ = split_row(iota((128, ROWS), 1))
    spread = jnp.where(x == iota((128, ROWS), 0), 1.0, 0.0).astype(BF)
    slots = dot(slot.astype(BF), spread)
    _, group, want = split_row(iota((TALL, ROWS), 1))
    chosen = (slots == want.astype(F32)) & (group == (iota((TALL, ROWS), 0) >> 6))
    mix = [jnp.where(chosen, dot(g.astype(BF), spread), 0.0).astype(BF) for g in gates]
    mix = jnp.concatenate(mix, axis=0)
    mine = unpacked_columns(rows)
    columns[...] = mine
    hidden = whole[:, :, FEAT:SEND].reshape(TALL, HSQ)
    shared = dot(hidden, mine, ((1,), (1,)))
    for i, out in enumerate((own, send1, send2, send3)):
        at = lax.rem(q + i, QS)
        piece = jnp.concatenate(
            [
                rows[d, e * QS + at].astype(F32)
                for d in range(DESTS)
                for e in range(HERE)
            ],
            axis=0,
        ).astype(BF)
        value = dot(mix, piece)
        value = value[:TALL] + value[TALL : 2 * TALL] + value[2 * TALL :]
        value += jnp.where(at == me, shared, 0.0)
        out[...] = value.reshape(ZHI, TOK, FEAT).astype(BF)


def zsum_kernel(got0, got1, got2, got3, columns, cot0, cot1, cot2, cot3, own, *outs):
    me = lax.axis_index("zhi")
    q = lax.axis_index("tensor")
    where = lax.rem(me - q + QS, QS)
    for k in range(ZHI):
        at = lax.rem(me + k, ZHI)
        value = sum(got[at].astype(F32) for got in (got0, got1, got2, got3))
        out = own if k == 0 else outs[k - 1]
        out[:, :FEAT] = value.astype(out.dtype)
    for i, cot in enumerate((cot0, cot1, cot2, cot3)):

        @pl.when(where == i)
        def _(cot=cot):
            for k in range(ZHI):
                out = own if k == 0 else outs[k - 1]
                part = dot(cot[lax.rem(me + k, ZHI)], columns[...])
                out[:, FEAT:] = part.astype(out.dtype)


def last_kernel(own, got1, got2, got3, layer, grad):
    value = own[...] + got1[...].astype(F32) + got2[...].astype(F32) + got3[...].astype(F32)
    layer[...] = value[:, :FEAT].astype(BF)
    grad[...] = value[:, FEAT:].astype(BF)


def moved(value, axes, count, step):
    return lax.ppermute(value, axes, [(i, (i + step) % count) for i in range(count)])


def z_pairs(step):
    total = ZHI * QS
    if step == 2:
        return [(z, (z + (2 if z % 2 == 0 else -2)) % total) for z in range(total)]
    return [(z, (z + step) % total) for z in range(total)]


def over_z(value, step):
    return lax.ppermute(value, ("zhi", "tensor"), z_pairs(step))


def over_z_and_phase(value, step):
    total = ZHI * QS
    pairs = [
        (p * total + a, (p + 1) % 4 * total + b) for p in range(4) for a, b in z_pairs(step)
    ]
    return lax.ppermute(value, ("phase", "zhi", "tensor"), pairs)


def bf16_parts(gates):
    first = lax.reduce_precision(gates, 8, 7)
    rest = gates - first
    second = lax.reduce_precision(rest, 8, 7)
    return [first, second, rest - second]


def on_device(
    forward_routes,
    forward_gates,
    hidden_rows,
    down_weight,
    shared_hidden,
    shared_weight,
    backward_routes,
    backward_gates,
    cotangent,
):
    weight = down_weight[0]
    cot = cotangent[0]
    meta = jnp.concatenate(
        [forward_routes[0].T.astype(F32), backward_routes[0].T.astype(F32)]
        + bf16_parts(forward_gates[0].T)
        + bf16_parts(backward_gates[0].T),
        axis=0,
    ).astype(BF)
    meta = jnp.pad(meta.T, ((0, 0), (0, 128 - 8 * TOP)))
    packed = jnp.concatenate([cot, shared_hidden[0], meta], axis=1)

    hidden = jnp.transpose(hidden_rows[0], (0, 2, 1, 3))
    parts = pl.pallas_call(
        fore_kernel,
        grid=(2 * HERE + 1,),
        in_specs=[
            pl.BlockSpec((1, MOST, ZHI * DESTS, HID), lambda i: (jnp.minimum(i // 2, 2), 0, 0, 0)),
            pl.BlockSpec(
                (1, HID, 2 * FEAT),
                lambda i: (jnp.minimum(i // 2, 2), 0, jnp.where(i < 6, lax.rem(i, 2), 1)),
            ),
            pl.BlockSpec((WCOL, HSQ), lambda i: (0, 0)),
        ],
        out_specs=pl.BlockSpec((DESTS, 2, SLOTS, FEAT), lambda i: (0, i, 0, 0)),
        out_shape=jax.ShapeDtypeStruct((DESTS, BLOCKS, SLOTS, FEAT), BF),
        scratch_shapes=[pltpu.VMEM((MOST * ZHI * DESTS, HID), BF)],
        cost_estimate=pl.CostEstimate(
            flops=2 * HERE * 192 * HID * FEAT * QS, bytes_accessed=8 * 10**6, transcendentals=0
        ),
        compiler_params=pltpu.CompilerParams(vmem_limit_bytes=40 * 2**20),
        name="expert_rows",
    )(hidden, weight, shared_weight[0].T)
    arrived = lax.all_to_all(parts, ("y", "core"), 0, 0, tiled=True)

    packed, parts = lax.optimization_barrier((packed, parts))
    whole = lax.all_gather(packed, "zhi", axis=0, tiled=False)
    held = whole[:, :, :FEAT]
    chunks = [held, over_z(held, -1), over_z(held, 2), over_z(held, 1)]
    [outgoing] = call(
        select_kernel,
        [((DESTS, HERE, QS, SLOTS, FEAT), BF)],
        [whole, *chunks],
        flops=2 * ROWS * TALL * FEAT * QS,
        name="select_rows",
    )
    received = lax.all_to_all(outgoing, ("y", "core"), 0, 0, tiled=True)

    chunk = ((ZHI, TOK, FEAT), BF)
    *sends, columns = call(
        combine_kernel,
        [chunk, chunk, chunk, chunk, ((FEAT, HSQ), BF)],
        [whole, arrived],
        flops=6 * TALL * ROWS * FEAT * QS,
        name="combine",
    )
    got = [over_z_and_phase(value, step) for value, step in zip(sends, (0, 1, 2, -1))]
    own, *sums = call(
        zsum_kernel,
        [((TOK, SEND), F32)] + [((TOK, SEND), BF)] * 3,
        [*got, columns, *chunks],
        name="z_sum",
    )
    last = [moved(value, "zhi", ZHI, k) for k, value in zip((1, 2, 3), sums)]
    handed, shared_back = call(
        last_kernel, [((TOK, FEAT), BF), ((TOK, HSQ), BF)], [own, *last], name="last_sum"
    )

    hidden_back = pl.pallas_call(
        back_kernel,
        grid=(HERE,),
        in_specs=[
            pl.BlockSpec((DESTS, 1, QS, SLOTS, FEAT), lambda e: (0, e, 0, 0, 0)),
            pl.BlockSpec((1, HID, FEAT * QS), lambda e: (e, 0, 0)),
        ],
        out_specs=pl.BlockSpec((1, MOST, ZHI * DESTS, HID), lambda e: (e, 0, 0, 0)),
        out_shape=jax.ShapeDtypeStruct((HERE, MOST, ZHI * DESTS, HID), BF),
        cost_estimate=pl.CostEstimate(
            flops=2 * HERE * 192 * HID * FEAT * QS, bytes_accessed=7 * 10**6, transcendentals=0
        ),
        compiler_params=pltpu.CompilerParams(vmem_limit_bytes=40 * 2**20),
        name="hidden_back",
    )(received, weight)
    return (
        handed[None],
        jnp.transpose(hidden_back, (0, 2, 1, 3))[None],
        shared_back[None],
    )


def solution(mesh):
    inner = Mesh(
        mesh.devices.reshape(4, ZHI, YS, CORES, QS), ("phase", "zhi", "y", "core", "tensor")
    )
    expert = ("zhi", "y", "core")
    return jax.shard_map(
        on_device,
        mesh=inner,
        in_specs=(
            P("phase", expert, None),
            P("phase", expert, None),
            P("phase", expert, None, None, "tensor"),
            P("phase", expert, "tensor", None),
            P("phase", expert, "tensor"),
            P("phase", "tensor", expert),
            P("phase", expert, None),
            P("phase", expert, None),
            P("phase", expert, "tensor"),
        ),
        out_specs=(
            P("phase", expert, "tensor"),
            P("phase", expert, None, None, "tensor"),
            P("phase", expert, "tensor"),
        ),
        check_vma=False,
    )
```

```python
import functools

import jax
import jax.numpy as jnp
from jax import lax
from jax.experimental import pallas as pl
from jax.experimental.pallas import tpu as pltpu
from jax.sharding import Mesh, PartitionSpec as P

BF, F32 = jnp.bfloat16, jnp.float32
ZHI, YS, CORES, QS = 4, 4, 2, 4
DESTS = YS * CORES
HERE, MOST, TOK, TOP = 3, 6, 64, 6
SLOTS = ZHI * MOST
COLS = DESTS * HERE
ROWS = COLS * SLOTS
FEAT, HID = 640, 256
HSQ, WCOL = 384, 80
TALL = ZHI * TOK
XPAD = 32
BLOCKS = HERE * QS + 2
SEND = FEAT + HSQ
VM = pl.BlockSpec(memory_space=pltpu.VMEM)


def call(body, outs, args, flops=0, name=None, vmem=8):
    out_shape = [jax.ShapeDtypeStruct(s, t) for s, t in outs]
    size = sum(a.size * a.dtype.itemsize for a in (*args, *out_shape))
    return pl.pallas_call(
        body,
        out_shape=out_shape,
        in_specs=[VM] * len(args),
        out_specs=[VM] * len(outs),
        cost_estimate=pl.CostEstimate(flops=flops, bytes_accessed=size, transcendentals=0),
        compiler_params=pltpu.CompilerParams(vmem_limit_bytes=vmem * 2**20),
        name=name,
    )(*args)


def iota(shape, dim):
    return lax.broadcasted_iota(jnp.int32, shape, dim)


def dot(a, b, dims=((1,), (0,))):
    return lax.dot_general(a, b, (dims, ((), ())), preferred_element_type=F32)


def split_row(r):
    x = (r * 2731) >> 16
    rest = r - x * SLOTS
    group = (rest * 43) >> 8
    return x, group, rest - group * MOST


def fore_kernel(
    hidden, weight, columns, routes, gates, back_routes, back_gates, cot, shared,
    out, packed, held, ready, meta_ref, weight_sems, out_sems,
):
    loads = [
        pltpu.make_async_copy(weight.at[e], held.at[e], weight_sems.at[e]) for e in range(HERE)
    ]
    for load in loads:
        load.start()

    def leave(at, size, which):
        return pltpu.make_async_copy(
            ready.at[:, pl.ds(at, size)], out.at[:, pl.ds(at, size)], out_sems.at[which]
        )

    wide = columns[...].astype(F32)
    tiles = [wide[8 * m : 8 * m + 8, 128 * i : 128 * i + 128] for i in range(3) for m in range(10)]
    for b in range(2):
        lanes = [jnp.concatenate(tiles[3 * n : 3 * n + 3], axis=0) for n in range(5 * b, 5 * b + 5)]
        block = jnp.concatenate(lanes, axis=1).astype(BF)
        for d in range(DESTS):
            ready[d, BLOCKS - 2 + b] = block
    leaving = [leave(BLOCKS - 2, 2, HERE)]
    leaving[0].start()

    meta_ref[...] = jnp.zeros(meta_ref.shape, F32)
    for k in range(TOP):
        meta_ref[k : k + 1, 0:TOK] = routes[k].astype(F32)
        meta_ref[8 + k : 9 + k, 0:TOK] = back_routes[k].astype(F32)
        for at, gate in ((16, gates), (40, back_gates)):
            rest = gate[k]
            for i in range(3):
                part = rest.astype(BF).astype(F32)
                meta_ref[at + 8 * i + k : at + 8 * i + k + 1, 0:TOK] = part
                rest = rest - part
    packed[:, :FEAT] = cot[...]
    packed[:, FEAT:SEND] = shared[...]
    packed[:, SEND:] = meta_ref[...].T[:TOK, :].astype(BF)

    count = MOST * ZHI * DESTS
    to, src = iota((count, count), 0), iota((count, count), 1)
    slot, group = src >> 5, src & 31
    zhi, dest = group >> 3, group & 7
    perm = jnp.where(to == (dest * SLOTS + zhi * MOST + slot), 1.0, 0.0).astype(BF)
    for e in range(HERE):
        rows = dot(perm, hidden[e].reshape(count, HID)).astype(BF)
        loads[e].wait()
        for q in range(QS):
            value = dot(rows, held[e, :, q * FEAT : (q + 1) * FEAT])
            ready[:, e * QS + q] = value.reshape(DESTS, SLOTS, FEAT).astype(BF)
        leaving.append(leave(e * QS, QS, e))
        leaving[-1].start()
    for copy in leaving:
        copy.wait()


def back_kernel(rows, weight, out, got, held, row_sems, weight_sems):
    loads = []
    for e in range(HERE):
        loads.append(pltpu.make_async_copy(rows.at[:, e], got.at[e], row_sems.at[e]))
        loads.append(pltpu.make_async_copy(weight.at[e], held.at[e], weight_sems.at[e]))
    for load in loads:
        load.start()
    count = MOST * ZHI * DESTS
    to, src = iota((count, count), 0), iota((count, count), 1)
    slot, group = to >> 5, to & 31
    zhi, dest = group >> 3, group & 7
    perm = jnp.where(src == (dest * SLOTS + zhi * MOST + slot), 1.0, 0.0).astype(BF)
    for e in range(HERE):
        loads[2 * e].wait()
        loads[2 * e + 1].wait()
        total = jnp.zeros((count, HID), F32)
        for q in range(QS):
            piece = got[e, :, q].astype(F32).reshape(count, FEAT).astype(BF)
            total += dot(piece, held[e, :, q * FEAT : (q + 1) * FEAT], ((1,), (1,)))
        value = dot(perm, total.astype(BF)).astype(BF)
        out[e] = value.reshape(MOST, ZHI * DESTS, HID)


def unpacked_columns(rows):
    pieces = []
    for d in range(DESTS):
        blocks = [rows[d, BLOCKS - 2 + b].astype(F32) for b in range(2)]
        tiles = [
            blocks[n // 5][8 * m : 8 * m + 8, 128 * (n % 5) : 128 * (n % 5) + 128]
            for n in range(10)
            for m in range(3)
        ]
        lanes = [jnp.concatenate(tiles[10 * i : 10 * i + 10], axis=0) for i in range(3)]
        pieces.append(jnp.concatenate(lanes, axis=1))
    return jnp.concatenate(pieces, axis=0).astype(BF)


def select_kernel(whole, columns, cot0, cot1, cot2, cot3, out, grads):
    q = lax.axis_index("tensor")
    me = lax.axis_index("zhi")
    meta = whole[:, :, SEND:].astype(F32).reshape(TALL, 128).T
    names = iota((XPAD, TALL), 0) + me * COLS
    hit = jnp.zeros((XPAD, TALL), F32)
    gates = [jnp.zeros((XPAD, TALL), F32) for _ in range(3)]
    for k in range(TOP):
        found = jnp.where(meta[8 + k : 9 + k, :].astype(jnp.int32) == names, 1.0, 0.0)
        hit += found
        for i in range(3):
            gates[i] += found * meta[40 + 8 * i + k : 41 + 8 * i + k, :]
    a, b = iota((TALL, TALL), 0), iota((TALL, TALL), 1)
    before = jnp.where((a < b) & ((a >> 6) == (b >> 6)), 1.0, 0.0).astype(BF)
    slot = jnp.where(hit > 0, dot(hit.astype(BF), before), 100.0)
    x, _, _ = split_row(iota((ROWS, XPAD), 0))
    spread = jnp.where(x == iota((ROWS, XPAD), 1), 1.0, 0.0).astype(BF)
    slots = dot(spread, slot.astype(BF))
    gate = sum(dot(spread, g.astype(BF)) for g in gates)
    _, group, want = split_row(iota((ROWS, TALL), 0))
    chosen = (slots == want.astype(F32)) & (group == (iota((ROWS, TALL), 1) >> 6))
    pick = jnp.where(chosen, 1.0, 0.0).astype(BF)
    scale = jnp.sum(jnp.where(chosen, gate, 0.0), axis=1, keepdims=True)
    for i, cot in enumerate((cot0, cot1, cot2, cot3)):
        at = lax.rem(q + i, QS)
        here = cot[...].reshape(TALL, FEAT)
        value = dot(pick, here) * scale
        out[:, :, at] = value.reshape(DESTS, HERE, SLOTS, FEAT).astype(BF)

        @pl.when(at == me)
        def _(here=here):
            grads[...] = dot(here, columns[...]).reshape(ZHI, TOK, HSQ)


def combine_kernel(whole, rows, own, send1, send2, send3, columns):
    me = lax.axis_index("zhi")
    q = lax.axis_index("tensor")
    meta = whole[:, :, SEND:].astype(F32).reshape(TALL, 128)
    names = iota((TALL, 128), 1) + me * COLS
    hit = jnp.zeros((TALL, 128), F32)
    gates = [jnp.zeros((TALL, 128), F32) for _ in range(3)]
    for k in range(TOP):
        found = jnp.where(meta[:, k : k + 1].astype(jnp.int32) == names, 1.0, 0.0)
        hit += found
        for i in range(3):
            gates[i] += found * meta[:, 16 + 8 * i + k : 17 + 8 * i + k]
    a, b = iota((TALL, TALL), 0), iota((TALL, TALL), 1)
    before = jnp.where((b < a) & ((a >> 6) == (b >> 6)), 1.0, 0.0).astype(BF)
    slot = jnp.where(hit > 0, dot(before, hit.astype(BF)), 100.0)
    x, _, _ = split_row(iota((128, ROWS), 1))
    spread = jnp.where(x == iota((128, ROWS), 0), 1.0, 0.0).astype(BF)
    slots = dot(slot.astype(BF), spread)
    _, group, want = split_row(iota((TALL, ROWS), 1))
    chosen = (slots == want.astype(F32)) & (group == (iota((TALL, ROWS), 0) >> 6))
    mix = [jnp.where(chosen, dot(g.astype(BF), spread), 0.0).astype(BF) for g in gates]
    mix = jnp.concatenate(mix, axis=0)
    mine = unpacked_columns(rows)
    columns[...] = mine
    hidden = whole[:, :, FEAT:SEND].reshape(TALL, HSQ)
    shared = dot(hidden, mine, ((1,), (1,)))
    for i, out in enumerate((own, send1, send2, send3)):
        at = lax.rem(q + i, QS)
        piece = jnp.concatenate(
            [
                rows[d, e * QS + at].astype(F32)
                for d in range(DESTS)
                for e in range(HERE)
            ],
            axis=0,
        ).astype(BF)
        value = dot(mix, piece)
        value = value[:TALL] + value[TALL : 2 * TALL] + value[2 * TALL :]
        value += jnp.where(at == me, shared, 0.0)
        out[...] = value.reshape(ZHI, TOK, FEAT).astype(out.dtype)


def zsum_kernel(got0, got1, got2, got3, grads, own, *outs):
    me = lax.axis_index("zhi")
    for k in range(ZHI):
        at = lax.rem(me + k, ZHI)
        value = sum(got[at].astype(F32) for got in (got0, got1, got2, got3))
        out = own if k == 0 else outs[k - 1]
        out[:, :FEAT] = value.astype(out.dtype)
        out[:, FEAT:] = grads[at].astype(out.dtype)


def last_kernel(own, got1, got2, got3, layer, grad):
    value = own[...] + got1[...].astype(F32) + got2[...].astype(F32) + got3[...].astype(F32)
    layer[...] = value[:, :FEAT].astype(BF)
    grad[...] = value[:, FEAT:].astype(BF)


def moved(value, axes, count, step):
    return lax.ppermute(value, axes, [(i, (i + step) % count) for i in range(count)])


def z_pairs(step):
    total = ZHI * QS
    if step == 2:
        return [(z, (z + (2 if z % 2 == 0 else -2)) % total) for z in range(total)]
    return [(z, (z + step) % total) for z in range(total)]


def over_z(value, step):
    return lax.ppermute(value, ("zhi", "tensor"), z_pairs(step))


def on_device(
    forward_routes,
    forward_gates,
    hidden_rows,
    down_weight,
    shared_hidden,
    shared_weight,
    backward_routes,
    backward_gates,
    cotangent,
):
    weight = down_weight[0]
    hidden = jnp.transpose(hidden_rows[0], (0, 2, 1, 3))
    small = [
        jnp.transpose(a, (2, 0, 1))
        for a in (forward_routes, forward_gates, backward_routes, backward_gates)
    ]
    anywhere = pl.BlockSpec(memory_space=pl.ANY)
    product = 2 * HERE * 192 * HID * FEAT * QS
    parts, packed = pl.pallas_call(
        fore_kernel,
        in_specs=[VM, anywhere] + [VM] * 7,
        out_specs=[anywhere, VM],
        out_shape=[
            jax.ShapeDtypeStruct((DESTS, BLOCKS, SLOTS, FEAT), BF),
            jax.ShapeDtypeStruct((TOK, SEND + 128), BF),
        ],
        scratch_shapes=[
            pltpu.VMEM((HERE, HID, QS * FEAT), BF),
            pltpu.VMEM((DESTS, BLOCKS, SLOTS, FEAT), BF),
            pltpu.VMEM((128, 128), F32),
            pltpu.SemaphoreType.DMA((HERE,)),
            pltpu.SemaphoreType.DMA((HERE + 1,)),
        ],
        cost_estimate=pl.CostEstimate(flops=product, bytes_accessed=8 * 10**6, transcendentals=0),
        compiler_params=pltpu.CompilerParams(vmem_limit_bytes=58 * 2**20),
        name="expert_rows",
    )(hidden, weight, shared_weight[0].T, *small, cotangent[0], shared_hidden[0])
    arrived = lax.all_to_all(parts, ("y", "core"), 0, 0, tiled=True)

    whole = lax.all_gather(packed, "zhi", axis=0, tiled=False)
    held = whole[:, :, :FEAT]
    chunks = [held, over_z(held, -1), over_z(held, 2), over_z(held, 1)]

    chunk = ((ZHI, TOK, FEAT), BF)
    own, *sends, columns = call(
        combine_kernel,
        [((ZHI, TOK, FEAT), F32), chunk, chunk, chunk, ((FEAT, HSQ), BF)],
        [whole, arrived],
        flops=6 * TALL * ROWS * FEAT * QS,
        name="combine",
        vmem=14,
    )
    got = [over_z(value, step) for value, step in zip(sends, (1, 2, -1))]

    outgoing, grads = call(
        select_kernel,
        [((DESTS, HERE, QS, SLOTS, FEAT), BF), ((ZHI, TOK, HSQ), F32)],
        [whole, columns, *chunks],
        flops=2 * ROWS * TALL * FEAT * QS,
        name="select_rows",
        vmem=14,
    )
    outgoing, *got = lax.optimization_barrier((outgoing, *got))
    received = lax.all_to_all(outgoing, ("y", "core"), 0, 0, tiled=True)

    own, *sums = call(
        zsum_kernel,
        [((TOK, SEND), F32)] + [((TOK, SEND), BF)] * 3,
        [own, *got, grads],
        name="z_sum",
    )
    last = [moved(value, "zhi", ZHI, k) for k, value in zip((1, 2, 3), sums)]
    hidden_back = pl.pallas_call(
        back_kernel,
        in_specs=[anywhere, anywhere],
        out_specs=VM,
        out_shape=jax.ShapeDtypeStruct((HERE, MOST, ZHI * DESTS, HID), BF),
        scratch_shapes=[
            pltpu.VMEM((HERE, DESTS, QS, SLOTS, FEAT), BF),
            pltpu.VMEM((HERE, HID, QS * FEAT), BF),
            pltpu.SemaphoreType.DMA((HERE,)),
            pltpu.SemaphoreType.DMA((HERE,)),
        ],
        cost_estimate=pl.CostEstimate(flops=product, bytes_accessed=7 * 10**6, transcendentals=0),
        compiler_params=pltpu.CompilerParams(vmem_limit_bytes=58 * 2**20),
        name="hidden_back",
    )(received, weight)
    own, hidden_back = lax.optimization_barrier((own, hidden_back))
    layer, shared_back = call(
        last_kernel, [((TOK, FEAT), BF), ((TOK, HSQ), BF)], [own, *last], name="last_sum"
    )
    handed = moved(layer, "phase", 4, 1)

    return (
        handed[None],
        jnp.transpose(hidden_back, (0, 2, 1, 3))[None],
        shared_back[None],
    )


def solution(mesh):
    inner = Mesh(
        mesh.devices.reshape(4, ZHI, YS, CORES, QS), ("phase", "zhi", "y", "core", "tensor")
    )
    expert = ("zhi", "y", "core")
    return jax.shard_map(
        on_device,
        mesh=inner,
        in_specs=(
            P("phase", expert, None),
            P("phase", expert, None),
            P("phase", expert, None, None, "tensor"),
            P("phase", expert, "tensor", None),
            P("phase", expert, "tensor"),
            P("phase", "tensor", expert),
            P("phase", expert, None),
            P("phase", expert, None),
            P("phase", expert, "tensor"),
        ),
        out_specs=(
            P("phase", expert, "tensor"),
            P("phase", expert, None, None, "tensor"),
            P("phase", expert, "tensor"),
        ),
        check_vma=False,
    )
```

```python
import functools

import jax
import jax.numpy as jnp
from jax import lax
from jax.experimental import pallas as pl
from jax.experimental.pallas import tpu as pltpu
from jax.sharding import Mesh, PartitionSpec as P

BF, F32 = jnp.bfloat16, jnp.float32
ZHI, YS, CORES, QS = 4, 4, 2, 4
DESTS = YS * CORES
HERE, MOST, TOK, TOP = 3, 6, 64, 6
SLOTS = ZHI * MOST
COLS = DESTS * HERE
ROWS = COLS * SLOTS
FEAT, HID = 640, 256
HSQ, WCOL = 384, 80
TALL = ZHI * TOK
XPAD = 32
BLOCKS = HERE * QS + 2
SEND = FEAT + HSQ
VM = pl.BlockSpec(memory_space=pltpu.VMEM)


def call(body, outs, args, flops=0, name=None, vmem=8):
    out_shape = [jax.ShapeDtypeStruct(s, t) for s, t in outs]
    size = sum(a.size * a.dtype.itemsize for a in (*args, *out_shape))
    return pl.pallas_call(
        body,
        out_shape=out_shape,
        in_specs=[VM] * len(args),
        out_specs=[VM] * len(outs),
        cost_estimate=pl.CostEstimate(flops=flops, bytes_accessed=size, transcendentals=0),
        compiler_params=pltpu.CompilerParams(vmem_limit_bytes=vmem * 2**20),
        name=name,
    )(*args)


def iota(shape, dim):
    return lax.broadcasted_iota(jnp.int32, shape, dim)


def dot(a, b, dims=((1,), (0,))):
    return lax.dot_general(a, b, (dims, ((), ())), preferred_element_type=F32)


def split_row(r):
    x = (r * 2731) >> 16
    rest = r - x * SLOTS
    group = (rest * 43) >> 8
    return x, group, rest - group * MOST


def fore_kernel(
    hidden, weight, columns, routes, gates, back_routes, back_gates, cot, shared,
    out, packed, held, ready, meta_ref, weight_sems, out_sems,
):
    loads = [
        pltpu.make_async_copy(weight.at[e], held.at[e], weight_sems.at[e]) for e in range(HERE)
    ]
    for load in loads:
        load.start()

    def leave(at, size, which):
        return pltpu.make_async_copy(
            ready.at[:, pl.ds(at, size)], out.at[:, pl.ds(at, size)], out_sems.at[which]
        )

    wide = columns[...].astype(F32)
    tiles = [wide[8 * m : 8 * m + 8, 128 * i : 128 * i + 128] for i in range(3) for m in range(10)]
    for b in range(2):
        lanes = [jnp.concatenate(tiles[3 * n : 3 * n + 3], axis=0) for n in range(5 * b, 5 * b + 5)]
        block = jnp.concatenate(lanes, axis=1).astype(BF)
        for d in range(DESTS):
            ready[d, BLOCKS - 2 + b] = block
    leaving = [leave(BLOCKS - 2, 2, HERE)]
    leaving[0].start()

    meta_ref[...] = jnp.zeros(meta_ref.shape, F32)
    for k in range(TOP):
        meta_ref[k : k + 1, 0:TOK] = routes[k].astype(F32)
        meta_ref[8 + k : 9 + k, 0:TOK] = back_routes[k].astype(F32)
        for at, gate in ((16, gates), (40, back_gates)):
            rest = gate[k]
            for i in range(3):
                part = rest.astype(BF).astype(F32)
                meta_ref[at + 8 * i + k : at + 8 * i + k + 1, 0:TOK] = part
                rest = rest - part
    packed[:, :FEAT] = cot[...]
    packed[:, FEAT:SEND] = shared[...]
    packed[:, SEND:] = meta_ref[...].T[:TOK, :].astype(BF)

    count = MOST * ZHI * DESTS
    to, src = iota((count, count), 0), iota((count, count), 1)
    slot, group = src >> 5, src & 31
    zhi, dest = group >> 3, group & 7
    perm = jnp.where(to == (dest * SLOTS + zhi * MOST + slot), 1.0, 0.0).astype(BF)
    for e in range(HERE):
        rows = dot(perm, hidden[e].reshape(count, HID)).astype(BF)
        loads[e].wait()
        for q in range(QS):
            value = dot(rows, held[e, :, q * FEAT : (q + 1) * FEAT])
            ready[:, e * QS + q] = value.reshape(DESTS, SLOTS, FEAT).astype(BF)
        leaving.append(leave(e * QS, QS, e))
        leaving[-1].start()
    for copy in leaving:
        copy.wait()


def back_kernel(rows, weight, out, got, held, row_sems, weight_sems):
    loads = []
    for e in range(HERE):
        loads.append(pltpu.make_async_copy(rows.at[:, e], got.at[e], row_sems.at[e]))
        loads.append(pltpu.make_async_copy(weight.at[e], held.at[e], weight_sems.at[e]))
    for load in loads:
        load.start()
    count = MOST * ZHI * DESTS
    to, src = iota((count, count), 0), iota((count, count), 1)
    slot, group = to >> 5, to & 31
    zhi, dest = group >> 3, group & 7
    perm = jnp.where(src == (dest * SLOTS + zhi * MOST + slot), 1.0, 0.0).astype(BF)
    for e in range(HERE):
        loads[2 * e].wait()
        loads[2 * e + 1].wait()
        total = jnp.zeros((count, HID), F32)
        for q in range(QS):
            piece = got[e, :, q].astype(F32).reshape(count, FEAT).astype(BF)
            total += dot(piece, held[e, :, q * FEAT : (q + 1) * FEAT], ((1,), (1,)))
        value = dot(perm, total.astype(BF)).astype(BF)
        out[e] = value.reshape(MOST, ZHI * DESTS, HID)


def unpacked_columns(rows):
    pieces = []
    for d in range(DESTS):
        blocks = [rows[d, BLOCKS - 2 + b].astype(F32) for b in range(2)]
        tiles = [
            blocks[n // 5][8 * m : 8 * m + 8, 128 * (n % 5) : 128 * (n % 5) + 128]
            for n in range(10)
            for m in range(3)
        ]
        lanes = [jnp.concatenate(tiles[10 * i : 10 * i + 10], axis=0) for i in range(3)]
        pieces.append(jnp.concatenate(lanes, axis=1))
    return jnp.concatenate(pieces, axis=0).astype(BF)


def select_kernel(whole, columns, cot0, cot1, cot2, cot3, out, grads):
    q = lax.axis_index("tensor")
    me = lax.axis_index("zhi")
    meta = whole[:, :, SEND:].astype(F32).reshape(TALL, 128).T
    names = iota((XPAD, TALL), 0) + me * COLS
    hit = jnp.zeros((XPAD, TALL), F32)
    gates = [jnp.zeros((XPAD, TALL), F32) for _ in range(3)]
    for k in range(TOP):
        found = jnp.where(meta[8 + k : 9 + k, :].astype(jnp.int32) == names, 1.0, 0.0)
        hit += found
        for i in range(3):
            gates[i] += found * meta[40 + 8 * i + k : 41 + 8 * i + k, :]
    a, b = iota((TALL, TALL), 0), iota((TALL, TALL), 1)
    before = jnp.where((a < b) & ((a >> 6) == (b >> 6)), 1.0, 0.0).astype(BF)
    slot = jnp.where(hit > 0, dot(hit.astype(BF), before), 100.0)
    x, _, _ = split_row(iota((ROWS, XPAD), 0))
    spread = jnp.where(x == iota((ROWS, XPAD), 1), 1.0, 0.0).astype(BF)
    slots = dot(spread, slot.astype(BF))
    gate = sum(dot(spread, g.astype(BF)) for g in gates)
    _, group, want = split_row(iota((ROWS, TALL), 0))
    chosen = (slots == want.astype(F32)) & (group == (iota((ROWS, TALL), 1) >> 6))
    pick = jnp.where(chosen, 1.0, 0.0).astype(BF)
    scale = jnp.sum(jnp.where(chosen, gate, 0.0), axis=1, keepdims=True)
    for i, cot in enumerate((cot0, cot1, cot2, cot3)):
        at = lax.rem(q + i, QS)
        here = cot[...].reshape(TALL, FEAT)
        value = dot(pick, here) * scale
        out[:, :, at] = value.reshape(DESTS, HERE, SLOTS, FEAT).astype(BF)

        @pl.when(at == me)
        def _(here=here):
            grads[...] = dot(here, columns[...]).reshape(ZHI, TOK, HSQ)


def combine_kernel(whole, rows, own, send1, send2, send3, columns):
    me = lax.axis_index("zhi")
    q = lax.axis_index("tensor")
    meta = whole[:, :, SEND:].astype(F32).reshape(TALL, 128)
    names = iota((TALL, 128), 1) + me * COLS
    hit = jnp.zeros((TALL, 128), F32)
    gates = [jnp.zeros((TALL, 128), F32) for _ in range(3)]
    for k in range(TOP):
        found = jnp.where(meta[:, k : k + 1].astype(jnp.int32) == names, 1.0, 0.0)
        hit += found
        for i in range(3):
            gates[i] += found * meta[:, 16 + 8 * i + k : 17 + 8 * i + k]
    a, b = iota((TALL, TALL), 0), iota((TALL, TALL), 1)
    before = jnp.where((b < a) & ((a >> 6) == (b >> 6)), 1.0, 0.0).astype(BF)
    slot = jnp.where(hit > 0, dot(before, hit.astype(BF)), 100.0)
    x, _, _ = split_row(iota((128, ROWS), 1))
    spread = jnp.where(x == iota((128, ROWS), 0), 1.0, 0.0).astype(BF)
    slots = dot(slot.astype(BF), spread)
    _, group, want = split_row(iota((TALL, ROWS), 1))
    chosen = (slots == want.astype(F32)) & (group == (iota((TALL, ROWS), 0) >> 6))
    mix = [jnp.where(chosen, dot(g.astype(BF), spread), 0.0).astype(BF) for g in gates]
    mix = jnp.concatenate(mix, axis=0)
    mine = unpacked_columns(rows)
    columns[...] = mine
    hidden = whole[:, :, FEAT:SEND].reshape(TALL, HSQ)
    shared = dot(hidden, mine, ((1,), (1,)))
    for i, out in enumerate((own, send1, send2, send3)):
        at = lax.rem(q + i, QS)
        piece = jnp.concatenate(
            [
                rows[d, e * QS + at].astype(F32)
                for d in range(DESTS)
                for e in range(HERE)
            ],
            axis=0,
        ).astype(BF)
        value = dot(mix, piece)
        value = value[:TALL] + value[TALL : 2 * TALL] + value[2 * TALL :]
        value += jnp.where(at == me, shared, 0.0)
        out[...] = value.reshape(ZHI, TOK, FEAT).astype(out.dtype)


def zsum_kernel(got0, got1, got2, got3, grads, own, held, far, near):
    me = lax.axis_index("zhi")
    step = 1 + 2 * lax.axis_index("core")
    for k, out in ((0, own), (step, held), (2, far), (ZHI - step, near)):
        at = lax.rem(me + k, ZHI)
        value = sum(got[at].astype(F32) for got in (got0, got1, got2, got3))
        out[:, :FEAT] = value.astype(out.dtype)
        out[:, FEAT:] = grads[at].astype(out.dtype)


def relay_kernel(held, passing, out):
    out[...] = (held[...] + passing[...].astype(F32)).astype(BF)


def last_kernel(own, got1, got2, layer, grad):
    value = own[...] + got1[...].astype(F32) + got2[...].astype(F32)
    layer[...] = value[:, :FEAT].astype(BF)
    grad[...] = value[:, FEAT:].astype(BF)


def ahead(value, sign):
    pairs = [
        (z * CORES + c, (z + sign * (1 - 2 * c)) % ZHI * CORES + c)
        for z in range(ZHI)
        for c in range(CORES)
    ]
    return lax.ppermute(value, ("zhi", "core"), pairs)


def moved(value, axes, count, step):
    return lax.ppermute(value, axes, [(i, (i + step) % count) for i in range(count)])


def z_pairs(step):
    total = ZHI * QS
    if step == 2:
        return [(z, (z + (2 if z % 2 == 0 else -2)) % total) for z in range(total)]
    return [(z, (z + step) % total) for z in range(total)]


def over_z(value, step):
    return lax.ppermute(value, ("zhi", "tensor"), z_pairs(step))


def on_device(
    forward_routes,
    forward_gates,
    hidden_rows,
    down_weight,
    shared_hidden,
    shared_weight,
    backward_routes,
    backward_gates,
    cotangent,
):
    weight = down_weight[0]
    hidden = jnp.transpose(hidden_rows[0], (0, 2, 1, 3))
    small = [
        jnp.transpose(a, (2, 0, 1))
        for a in (forward_routes, forward_gates, backward_routes, backward_gates)
    ]
    anywhere = pl.BlockSpec(memory_space=pl.ANY)
    product = 2 * HERE * 192 * HID * FEAT * QS
    parts, packed = pl.pallas_call(
        fore_kernel,
        in_specs=[VM, anywhere] + [VM] * 7,
        out_specs=[anywhere, VM],
        out_shape=[
            jax.ShapeDtypeStruct((DESTS, BLOCKS, SLOTS, FEAT), BF),
            jax.ShapeDtypeStruct((TOK, SEND + 128), BF),
        ],
        scratch_shapes=[
            pltpu.VMEM((HERE, HID, QS * FEAT), BF),
            pltpu.VMEM((DESTS, BLOCKS, SLOTS, FEAT), BF),
            pltpu.VMEM((128, 128), F32),
            pltpu.SemaphoreType.DMA((HERE,)),
            pltpu.SemaphoreType.DMA((HERE + 1,)),
        ],
        cost_estimate=pl.CostEstimate(flops=product, bytes_accessed=8 * 10**6, transcendentals=0),
        compiler_params=pltpu.CompilerParams(vmem_limit_bytes=58 * 2**20),
        name="expert_rows",
    )(hidden, weight, shared_weight[0].T, *small, cotangent[0], shared_hidden[0])
    arrived = lax.all_to_all(parts, ("y", "core"), 0, 0, tiled=True)

    whole = lax.all_gather(packed, "zhi", axis=0, tiled=False)
    held = whole[:, :, :FEAT]
    chunks = [held, over_z(held, -1), over_z(held, 2), over_z(held, 1)]

    chunk = ((ZHI, TOK, FEAT), BF)
    own, *sends, columns = call(
        combine_kernel,
        [((ZHI, TOK, FEAT), F32), chunk, chunk, chunk, ((FEAT, HSQ), BF)],
        [whole, arrived],
        flops=6 * TALL * ROWS * FEAT * QS,
        name="combine",
        vmem=14,
    )
    got = [over_z(value, step) for value, step in zip(sends, (1, 2, -1))]

    outgoing, grads = call(
        select_kernel,
        [((DESTS, HERE, QS, SLOTS, FEAT), BF), ((ZHI, TOK, HSQ), F32)],
        [whole, columns, *chunks],
        flops=2 * ROWS * TALL * FEAT * QS,
        name="select_rows",
        vmem=14,
    )
    outgoing, *got = lax.optimization_barrier((outgoing, *got))
    received = lax.all_to_all(outgoing, ("y", "core"), 0, 0, tiled=True)

    own, held, far, near = call(
        zsum_kernel,
        [((TOK, SEND), F32), ((TOK, SEND), F32), ((TOK, SEND), BF), ((TOK, SEND), BF)],
        [own, *got, grads],
        name="z_sum",
    )
    passing, near = ahead(far, 1), ahead(near, -1)
    [further] = call(relay_kernel, [((TOK, SEND), BF)], [held, passing], name="z_relay")
    last = [near, ahead(further, 1)]
    layer, shared_back = call(
        last_kernel, [((TOK, FEAT), BF), ((TOK, HSQ), BF)], [own, *last], name="last_sum"
    )
    handed = moved(layer, "phase", 4, 1)

    layer, received = lax.optimization_barrier((layer, received))
    hidden_back = pl.pallas_call(
        back_kernel,
        in_specs=[anywhere, anywhere],
        out_specs=VM,
        out_shape=jax.ShapeDtypeStruct((HERE, MOST, ZHI * DESTS, HID), BF),
        scratch_shapes=[
            pltpu.VMEM((HERE, DESTS, QS, SLOTS, FEAT), BF),
            pltpu.VMEM((HERE, HID, QS * FEAT), BF),
            pltpu.SemaphoreType.DMA((HERE,)),
            pltpu.SemaphoreType.DMA((HERE,)),
        ],
        cost_estimate=pl.CostEstimate(flops=product, bytes_accessed=7 * 10**6, transcendentals=0),
        compiler_params=pltpu.CompilerParams(vmem_limit_bytes=58 * 2**20),
        name="hidden_back",
    )(received, weight)
    return (
        handed[None],
        jnp.transpose(hidden_back, (0, 2, 1, 3))[None],
        shared_back[None],
    )


def solution(mesh):
    inner = Mesh(
        mesh.devices.reshape(4, ZHI, YS, CORES, QS), ("phase", "zhi", "y", "core", "tensor")
    )
    expert = ("zhi", "y", "core")
    return jax.shard_map(
        on_device,
        mesh=inner,
        in_specs=(
            P("phase", expert, None),
            P("phase", expert, None),
            P("phase", expert, None, None, "tensor"),
            P("phase", expert, "tensor", None),
            P("phase", expert, "tensor"),
            P("phase", "tensor", expert),
            P("phase", expert, None),
            P("phase", expert, None),
            P("phase", expert, "tensor"),
        ),
        out_specs=(
            P("phase", expert, "tensor"),
            P("phase", expert, None, None, "tensor"),
            P("phase", expert, "tensor"),
        ),
        check_vma=False,
    )
```

```python
import functools

import jax
import jax.numpy as jnp
from jax import lax
from jax.experimental import pallas as pl
from jax.experimental.pallas import tpu as pltpu
from jax.sharding import Mesh, PartitionSpec as P

BF, F32 = jnp.bfloat16, jnp.float32
ZHI, YS, CORES, QS = 4, 4, 2, 4
DESTS = YS * CORES
HERE, MOST, TOK, TOP = 3, 6, 64, 6
SLOTS = ZHI * MOST
COLS = DESTS * HERE
ROWS = COLS * SLOTS
FEAT, HID = 640, 256
HSQ, WCOL = 384, 80
TALL = ZHI * TOK
XPAD = 32
BLOCKS = HERE * QS + 2
SEND = FEAT + HSQ
VM = pl.BlockSpec(memory_space=pltpu.VMEM)


def call(body, outs, args, flops=0, name=None, vmem=8):
    out_shape = [jax.ShapeDtypeStruct(s, t) for s, t in outs]
    size = sum(a.size * a.dtype.itemsize for a in (*args, *out_shape))
    return pl.pallas_call(
        body,
        out_shape=out_shape,
        in_specs=[VM] * len(args),
        out_specs=[VM] * len(outs),
        cost_estimate=pl.CostEstimate(flops=flops, bytes_accessed=size, transcendentals=0),
        compiler_params=pltpu.CompilerParams(vmem_limit_bytes=vmem * 2**20),
        name=name,
    )(*args)


def iota(shape, dim):
    return lax.broadcasted_iota(jnp.int32, shape, dim)


def dot(a, b, dims=((1,), (0,))):
    return lax.dot_general(a, b, (dims, ((), ())), preferred_element_type=F32)


def split_row(r):
    x = (r * 2731) >> 16
    rest = r - x * SLOTS
    group = (rest * 43) >> 8
    return x, group, rest - group * MOST


def fore_kernel(
    hidden, weight, columns, routes, gates, back_routes, back_gates, cot, shared,
    out, packed, held, ready, meta_ref, weight_sems, out_sems,
):
    loads = [
        pltpu.make_async_copy(weight.at[e], held.at[e], weight_sems.at[e]) for e in range(HERE)
    ]
    for load in loads:
        load.start()

    def leave(at, size, which):
        return pltpu.make_async_copy(
            ready.at[:, pl.ds(at, size)], out.at[:, pl.ds(at, size)], out_sems.at[which]
        )

    wide = columns[...].astype(F32)
    tiles = [wide[8 * m : 8 * m + 8, 128 * i : 128 * i + 128] for i in range(3) for m in range(10)]
    for b in range(2):
        lanes = [jnp.concatenate(tiles[3 * n : 3 * n + 3], axis=0) for n in range(5 * b, 5 * b + 5)]
        block = jnp.concatenate(lanes, axis=1).astype(BF)
        for d in range(DESTS):
            ready[d, BLOCKS - 2 + b] = block
    leaving = [leave(BLOCKS - 2, 2, HERE)]
    leaving[0].start()

    meta_ref[...] = jnp.zeros(meta_ref.shape, F32)
    for k in range(TOP):
        meta_ref[k : k + 1, 0:TOK] = routes[k].astype(F32)
        meta_ref[8 + k : 9 + k, 0:TOK] = back_routes[k].astype(F32)
        for at, gate in ((16, gates), (40, back_gates)):
            rest = gate[k]
            for i in range(3):
                part = rest.astype(BF).astype(F32)
                meta_ref[at + 8 * i + k : at + 8 * i + k + 1, 0:TOK] = part
                rest = rest - part
    packed[:, :FEAT] = cot[...]
    packed[:, FEAT:SEND] = shared[...]
    packed[:, SEND:] = meta_ref[...].T[:TOK, :].astype(BF)

    count = MOST * ZHI * DESTS
    to, src = iota((count, count), 0), iota((count, count), 1)
    slot, group = src >> 5, src & 31
    zhi, dest = group >> 3, group & 7
    perm = jnp.where(to == (dest * SLOTS + zhi * MOST + slot), 1.0, 0.0).astype(BF)
    for e in range(HERE):
        rows = dot(perm, hidden[e].reshape(count, HID)).astype(BF)
        loads[e].wait()
        for q in range(QS):
            value = dot(rows, held[e, :, q * FEAT : (q + 1) * FEAT])
            ready[:, e * QS + q] = value.reshape(DESTS, SLOTS, FEAT).astype(BF)
        leaving.append(leave(e * QS, QS, e))
        leaving[-1].start()
    for copy in leaving:
        copy.wait()


def back_kernel(rows, weight, out, got, held, row_sems, weight_sems):
    loads = []
    for e in range(HERE):
        loads.append(pltpu.make_async_copy(rows.at[:, e], got.at[e], row_sems.at[e]))
        loads.append(pltpu.make_async_copy(weight.at[e], held.at[e], weight_sems.at[e]))
    for load in loads:
        load.start()
    count = MOST * ZHI * DESTS
    to, src = iota((count, count), 0), iota((count, count), 1)
    slot, group = to >> 5, to & 31
    zhi, dest = group >> 3, group & 7
    perm = jnp.where(src == (dest * SLOTS + zhi * MOST + slot), 1.0, 0.0).astype(BF)
    for e in range(HERE):
        loads[2 * e].wait()
        loads[2 * e + 1].wait()
        total = jnp.zeros((count, HID), F32)
        for q in range(QS):
            piece = got[e, :, q].astype(F32).reshape(count, FEAT).astype(BF)
            total += dot(piece, held[e, :, q * FEAT : (q + 1) * FEAT], ((1,), (1,)))
        value = dot(perm, total.astype(BF)).astype(BF)
        out[e] = value.reshape(MOST, ZHI * DESTS, HID)


def unpacked_columns(rows):
    pieces = []
    for d in range(DESTS):
        blocks = [rows[d, BLOCKS - 2 + b].astype(F32) for b in range(2)]
        tiles = [
            blocks[n // 5][8 * m : 8 * m + 8, 128 * (n % 5) : 128 * (n % 5) + 128]
            for n in range(10)
            for m in range(3)
        ]
        lanes = [jnp.concatenate(tiles[10 * i : 10 * i + 10], axis=0) for i in range(3)]
        pieces.append(jnp.concatenate(lanes, axis=1))
    return jnp.concatenate(pieces, axis=0).astype(BF)


def select_kernel(whole, columns, cot0, cot1, cot2, cot3, out, grads):
    q = lax.axis_index("tensor")
    me = lax.axis_index("zhi")
    meta = whole[:, :, SEND:].astype(F32).reshape(TALL, 128).T
    names = iota((XPAD, TALL), 0) + me * COLS
    hit = jnp.zeros((XPAD, TALL), F32)
    gates = [jnp.zeros((XPAD, TALL), F32) for _ in range(3)]
    for k in range(TOP):
        found = jnp.where(meta[8 + k : 9 + k, :].astype(jnp.int32) == names, 1.0, 0.0)
        hit += found
        for i in range(3):
            gates[i] += found * meta[40 + 8 * i + k : 41 + 8 * i + k, :]
    a, b = iota((TALL, TALL), 0), iota((TALL, TALL), 1)
    before = jnp.where((a < b) & ((a >> 6) == (b >> 6)), 1.0, 0.0).astype(BF)
    slot = jnp.where(hit > 0, dot(hit.astype(BF), before), 100.0)
    x, _, _ = split_row(iota((ROWS, XPAD), 0))
    spread = jnp.where(x == iota((ROWS, XPAD), 1), 1.0, 0.0).astype(BF)
    slots = dot(spread, slot.astype(BF))
    gate = sum(dot(spread, g.astype(BF)) for g in gates)
    _, group, want = split_row(iota((ROWS, TALL), 0))
    chosen = (slots == want.astype(F32)) & (group == (iota((ROWS, TALL), 1) >> 6))
    pick = jnp.where(chosen, 1.0, 0.0).astype(BF)
    scale = jnp.sum(jnp.where(chosen, gate, 0.0), axis=1, keepdims=True)
    for i, cot in enumerate((cot0, cot1, cot2, cot3)):
        at = lax.rem(q + i, QS)
        here = cot[...].reshape(TALL, FEAT)
        value = dot(pick, here) * scale
        out[:, :, at] = value.reshape(DESTS, HERE, SLOTS, FEAT).astype(BF)

        @pl.when(at == me)
        def _(here=here):
            grads[...] = dot(here, columns[...]).reshape(ZHI, TOK, HSQ)


def combine_kernel(whole, rows, own, send1, send2, send3, columns):
    me = lax.axis_index("zhi")
    q = lax.axis_index("tensor")
    meta = whole[:, :, SEND:].astype(F32).reshape(TALL, 128)
    names = iota((TALL, 128), 1) + me * COLS
    hit = jnp.zeros((TALL, 128), F32)
    gates = [jnp.zeros((TALL, 128), F32) for _ in range(3)]
    for k in range(TOP):
        found = jnp.where(meta[:, k : k + 1].astype(jnp.int32) == names, 1.0, 0.0)
        hit += found
        for i in range(3):
            gates[i] += found * meta[:, 16 + 8 * i + k : 17 + 8 * i + k]
    a, b = iota((TALL, TALL), 0), iota((TALL, TALL), 1)
    before = jnp.where((b < a) & ((a >> 6) == (b >> 6)), 1.0, 0.0).astype(BF)
    slot = jnp.where(hit > 0, dot(before, hit.astype(BF)), 100.0)
    x, _, _ = split_row(iota((128, ROWS), 1))
    spread = jnp.where(x == iota((128, ROWS), 0), 1.0, 0.0).astype(BF)
    slots = dot(slot.astype(BF), spread)
    _, group, want = split_row(iota((TALL, ROWS), 1))
    chosen = (slots == want.astype(F32)) & (group == (iota((TALL, ROWS), 0) >> 6))
    mix = [jnp.where(chosen, dot(g.astype(BF), spread), 0.0).astype(BF) for g in gates]
    mix = jnp.concatenate(mix, axis=0)
    mine = unpacked_columns(rows)
    columns[...] = mine
    hidden = whole[:, :, FEAT:SEND].reshape(TALL, HSQ)
    shared = dot(hidden, mine, ((1,), (1,)))
    for i, out in enumerate((own, send1, send2, send3)):
        at = lax.rem(q + i, QS)
        piece = jnp.concatenate(
            [
                rows[d, e * QS + at].astype(F32)
                for d in range(DESTS)
                for e in range(HERE)
            ],
            axis=0,
        ).astype(BF)
        value = dot(mix, piece)
        value = value[:TALL] + value[TALL : 2 * TALL] + value[2 * TALL :]
        value += jnp.where(at == me, shared, 0.0)
        out[...] = value.reshape(ZHI, TOK, FEAT).astype(out.dtype)


def zsum_kernel(got0, got1, got2, got3, grads, own, held, far, near):
    me = lax.axis_index("zhi")
    step = 1 + 2 * lax.axis_index("core")
    for k, out in ((0, own), (step, held), (2, far), (ZHI - step, near)):
        at = lax.rem(me + k, ZHI)
        value = sum(got[at].astype(F32) for got in (got0, got1, got2, got3))
        out[:, :FEAT] = value.astype(out.dtype)
        out[:, FEAT:] = grads[at].astype(out.dtype)


def relay_kernel(held, passing, out):
    out[...] = (held[...] + passing[...].astype(F32)).astype(BF)


def last_kernel(own, got1, got2, layer, grad):
    value = own[...] + got1[...].astype(F32) + got2[...].astype(F32)
    layer[...] = value[:, :FEAT].astype(BF)
    grad[...] = value[:, FEAT:].astype(BF)


def ahead(value, sign):
    pairs = [
        (z * CORES + c, (z + sign * (1 - 2 * c)) % ZHI * CORES + c)
        for z in range(ZHI)
        for c in range(CORES)
    ]
    return lax.ppermute(value, ("zhi", "core"), pairs)


def moved(value, axes, count, step):
    return lax.ppermute(value, axes, [(i, (i + step) % count) for i in range(count)])


def z_pairs(step):
    total = ZHI * QS
    if step == 2:
        return [(z, (z + (2 if z % 2 == 0 else -2)) % total) for z in range(total)]
    return [(z, (z + step) % total) for z in range(total)]


def over_z(value, step):
    return lax.ppermute(value, ("zhi", "tensor"), z_pairs(step))


def on_device(
    forward_routes,
    forward_gates,
    hidden_rows,
    down_weight,
    shared_hidden,
    shared_weight,
    backward_routes,
    backward_gates,
    cotangent,
):
    weight = down_weight[0]
    hidden = jnp.transpose(hidden_rows[0], (0, 2, 1, 3))
    small = [
        jnp.transpose(a, (2, 0, 1))
        for a in (forward_routes, forward_gates, backward_routes, backward_gates)
    ]
    anywhere = pl.BlockSpec(memory_space=pl.ANY)
    product = 2 * HERE * 192 * HID * FEAT * QS
    parts, packed = pl.pallas_call(
        fore_kernel,
        in_specs=[VM, anywhere] + [VM] * 7,
        out_specs=[anywhere, VM],
        out_shape=[
            jax.ShapeDtypeStruct((DESTS, BLOCKS, SLOTS, FEAT), BF),
            jax.ShapeDtypeStruct((TOK, SEND + 128), BF),
        ],
        scratch_shapes=[
            pltpu.VMEM((HERE, HID, QS * FEAT), BF),
            pltpu.VMEM((DESTS, BLOCKS, SLOTS, FEAT), BF),
            pltpu.VMEM((128, 128), F32),
            pltpu.SemaphoreType.DMA((HERE,)),
            pltpu.SemaphoreType.DMA((HERE + 1,)),
        ],
        cost_estimate=pl.CostEstimate(flops=product, bytes_accessed=8 * 10**6, transcendentals=0),
        compiler_params=pltpu.CompilerParams(vmem_limit_bytes=58 * 2**20),
        name="expert_rows",
    )(hidden, weight, shared_weight[0].T, *small, cotangent[0], shared_hidden[0])
    arrived = lax.all_to_all(parts, ("y", "core"), 0, 0, tiled=True)

    whole = lax.all_gather(packed, "zhi", axis=0, tiled=False)
    held = whole[:, :, :FEAT]
    chunks = [held, over_z(held, -1), over_z(held, 2), over_z(held, 1)]

    chunk = ((ZHI, TOK, FEAT), BF)
    own, *sends, columns = call(
        combine_kernel,
        [((ZHI, TOK, FEAT), F32), chunk, chunk, chunk, ((FEAT, HSQ), BF)],
        [whole, arrived],
        flops=6 * TALL * ROWS * FEAT * QS,
        name="combine",
        vmem=14,
    )
    got = [over_z(value, step) for value, step in zip(sends, (1, 2, -1))]

    outgoing, grads = call(
        select_kernel,
        [((DESTS, HERE, QS, SLOTS, FEAT), BF), ((ZHI, TOK, HSQ), F32)],
        [whole, columns, *chunks],
        flops=2 * ROWS * TALL * FEAT * QS,
        name="select_rows",
        vmem=14,
    )
    outgoing, got[0], got[1] = lax.optimization_barrier((outgoing, got[0], got[1]))
    received = lax.all_to_all(outgoing, ("y", "core"), 0, 0, tiled=True)

    own, held, far, near = call(
        zsum_kernel,
        [((TOK, SEND), F32), ((TOK, SEND), F32), ((TOK, SEND), BF), ((TOK, SEND), BF)],
        [own, *got, grads],
        name="z_sum",
    )
    passing, near = ahead(far, 1), ahead(near, -1)
    [further] = call(relay_kernel, [((TOK, SEND), BF)], [held, passing], name="z_relay")
    last = [near, ahead(further, 1)]
    layer, shared_back = call(
        last_kernel, [((TOK, FEAT), BF), ((TOK, HSQ), BF)], [own, *last], name="last_sum"
    )
    handed = moved(layer, "phase", 4, 1)

    layer, received = lax.optimization_barrier((layer, received))
    hidden_back = pl.pallas_call(
        back_kernel,
        in_specs=[anywhere, anywhere],
        out_specs=VM,
        out_shape=jax.ShapeDtypeStruct((HERE, MOST, ZHI * DESTS, HID), BF),
        scratch_shapes=[
            pltpu.VMEM((HERE, DESTS, QS, SLOTS, FEAT), BF),
            pltpu.VMEM((HERE, HID, QS * FEAT), BF),
            pltpu.SemaphoreType.DMA((HERE,)),
            pltpu.SemaphoreType.DMA((HERE,)),
        ],
        cost_estimate=pl.CostEstimate(flops=product, bytes_accessed=7 * 10**6, transcendentals=0),
        compiler_params=pltpu.CompilerParams(vmem_limit_bytes=58 * 2**20),
        name="hidden_back",
    )(received, weight)
    return (
        handed[None],
        jnp.transpose(hidden_back, (0, 2, 1, 3))[None],
        shared_back[None],
    )


def solution(mesh):
    inner = Mesh(
        mesh.devices.reshape(4, ZHI, YS, CORES, QS), ("phase", "zhi", "y", "core", "tensor")
    )
    expert = ("zhi", "y", "core")
    return jax.shard_map(
        on_device,
        mesh=inner,
        in_specs=(
            P("phase", expert, None),
            P("phase", expert, None),
            P("phase", expert, None, None, "tensor"),
            P("phase", expert, "tensor", None),
            P("phase", expert, "tensor"),
            P("phase", "tensor", expert),
            P("phase", expert, None),
            P("phase", expert, None),
            P("phase", expert, "tensor"),
        ),
        out_specs=(
            P("phase", expert, "tensor"),
            P("phase", expert, None, None, "tensor"),
            P("phase", expert, "tensor"),
        ),
        check_vma=False,
    )
```
